512 devices in a mesh: outer: 32 (over y_lo, z), inner: 16 (over x, y_hi, core).
Axes of the slice: x: 4, y: 4 (y_hi: 2, y_lo: 2; y = y_hi * 2 + y_lo), z: 16, core: 2. Of those that a mesh axis runs over, the one named last changes fastest.
Arguments:
- queries: bfloat16 [262144, 1024], P(('outer', 'inner')), may hold values from -6 to 6
- keys: bfloat16 [262144, 128], P(('outer', 'inner')), may hold values from -6 to 6
- values: bfloat16 [262144, 128], P(('outer', 'inner')), may hold values from -6 to 6
- doc_lengths: int32 [64], replicated, may hold values from 1 to 32768, 262144 in all
Outputs:
- attended: bfloat16 [262144, 1024], P(('outer', 'inner'))
- log_total: float32 [8, 262144], P(None, ('outer', 'inner'))
The draws below stay inside these ranges and needn't reach their ends.
Inputs may be any that keep to these rules, and one draw needn't show every extreme that they name: `doc_lengths`: the documents lie end to end from position 0 and fill the row; the longest has exactly 32768 positions.
All inputs are finite; a program needn't handle non-finite values.
Results may differ from the reference program's by a relative error of at most 0.0041.
Values may be sent and summed in bfloat16 or wider, within the bound.
No kernel may reach another device: no remote copies, remote signals or barrier semaphores. Data moves between devices by JAX's collectives and lax.ppermute only.
A program may use at most 64 MiB of HBM per device.

```python
import math
import jax
import jax.numpy as jnp
import numpy as np
from jax import lax

HEADS = 8
HEAD_DIM = 128
TOK_DEV = 512
STEPS = 3
DOCS = 64
WINDOW = 1536
SEQ = 262144
MOST = 32768
N_OUTER = 32
N_INNER = 16


def draw_queries(key, part):
    key = jax.random.fold_in(key, 11)
    base = jnp.clip(jax.random.normal(key, (SEQ, HEADS * HEAD_DIM), jnp.float32), -6.0, 6.0)
    return base.astype(jnp.bfloat16)


def draw_keys(key, part):
    key = jax.random.fold_in(key, 12)
    base = jnp.clip(jax.random.normal(key, (SEQ, HEAD_DIM), jnp.float32), -6.0, 6.0)
    return base.astype(jnp.bfloat16)


def steps_of(own_key, dims, pieces, smallest, top_value):
    def one(axis_at, blocks):
        draws = jax.random.uniform(jax.random.fold_in(jax.random.fold_in(own_key, 6), axis_at), (blocks,), jnp.float32, smallest / len(pieces), top_value / len(pieces))
        return jnp.repeat(jnp.exp(draws), dims[axis_at] // blocks).reshape((-1,) + (1,) * (len(dims) - axis_at - 1))

    gain = one(*pieces[0])
    for cut in pieces[1:]:
        gain = gain * one(*cut)
    return gain


def split_up(number_of, total, bound, skew):
    loads = [(1 << 20) // math.isqrt(rank ** skew) + 1 for rank in range(2, number_of + 1)]
    surplus, counts = total - bound - (number_of - 1), [1] * (number_of - 1)
    while surplus > 0:
        movable = [i for i in range(number_of - 1) if counts[i] < bound]
        whole, remaining = sum([loads[i] for i in movable]), surplus
        for i in movable:
            more = min(bound - counts[i], max(1, remaining * loads[i] // whole), surplus)
            counts[i] = counts[i] + more
            surplus = surplus - more
    return np.array([bound] + counts)


def uneven_parts(rng, amount, total, bound, lean):
    if amount == 2:
        one = jax.random.randint(rng, (), max(1, total - bound), min(bound, total - 1) + 1)
        return jnp.stack([one, total - one])
    sizes = jnp.asarray(split_up(amount, total, bound, lean), jnp.int32)
    couples = (amount - 1) // 2
    donor, taker = sizes[1:1 + 2 * couples:2], sizes[2:2 + 2 * couples:2]
    margin = jnp.minimum(donor - 1, bound - taker)
    moved = jax.random.randint(jax.random.fold_in(rng, 1), (couples,), 0, 1 << 20) % (margin + 1)
    sizes = sizes.at[1:1 + 2 * couples:2].set(donor - moved).at[2:2 + 2 * couples:2].set(taker + moved)
    return sizes[jax.random.permutation(jax.random.fold_in(rng, 2), amount)]


def centred(own_key, shape, scale, reach, shards=(), kind=jnp.bfloat16):
    values = scale * jax.random.normal(own_key, shape, jnp.float32)
    if shards:
        values = values * steps_of(own_key, shape, shards, -0.22, 0.18)
    return jnp.clip(values, -reach, reach).astype(kind)


def setup_inputs(seed: int = 0) -> dict:
    seeds = jax.random.split(jax.random.key(seed), 5)
    queries = draw_queries(jax.random.fold_in(seeds[4], 71), 0)
    keys = draw_keys(jax.random.fold_in(seeds[4], 71), 0)
    values = centred(seeds[2], (SEQ, HEAD_DIM), 1.0, 6.0, ((0, 512),))
    doc_lengths = uneven_parts(seeds[3], DOCS, SEQ, MOST, 2).astype(jnp.int32)
    return {"queries": queries, "keys": keys, "values": values, "doc_lengths": doc_lengths}


def reference(queries, keys, values, doc_lengths):
    devices = N_OUTER * N_INNER
    front = STEPS * TOK_DEV
    positions = jnp.arange(SEQ, dtype=jnp.int32)
    ends = jnp.cumsum(doc_lengths).astype(jnp.int32)
    doc = jnp.sum((positions[:, None] >= ends[None, :]).astype(jnp.int32), axis=1).astype(jnp.int32)
    key_pad = jnp.concatenate([jnp.zeros((front, HEAD_DIM), keys.dtype), keys], axis=0)
    value_pad = jnp.concatenate([jnp.zeros((front, HEAD_DIM), values.dtype), values], axis=0)
    pos_pad = jnp.concatenate([jnp.full((front,), -1, jnp.int32), positions]).astype(jnp.int32)
    doc_pad = jnp.concatenate([jnp.full((front,), -1, jnp.int32), doc]).astype(jnp.int32)
    scale = HEAD_DIM ** -0.5

    def one_device(dev):
        start = (dev * TOK_DEV).astype(jnp.int32)
        key_win = lax.dynamic_slice_in_dim(key_pad, start, front + TOK_DEV, 0).astype(jnp.float32)
        value_win = lax.dynamic_slice_in_dim(value_pad, start, front + TOK_DEV, 0).astype(jnp.float32)
        key_pos = lax.dynamic_slice_in_dim(pos_pad, start, front + TOK_DEV, 0)
        key_doc = lax.dynamic_slice_in_dim(doc_pad, start, front + TOK_DEV, 0)
        query_pos = lax.dynamic_slice_in_dim(positions, start, TOK_DEV, 0)
        query_doc = lax.dynamic_slice_in_dim(doc, start, TOK_DEV, 0)
        query_here = lax.dynamic_slice_in_dim(queries, start, TOK_DEV, 0).reshape(TOK_DEV, HEADS, HEAD_DIM).astype(jnp.float32)
        score = jnp.einsum("thd,kd->htk", query_here, key_win) * scale
        gap = query_pos[:, None] - key_pos[None, :]
        allowed = (key_pos[None, :] >= 0) & (gap >= 0) & (gap < WINDOW) & (key_doc[None, :] == query_doc[:, None])
        score = jnp.where(allowed[None], score, -jnp.inf)
        top = jnp.max(score, axis=2)
        expon = jnp.exp(score - top[:, :, None])
        total = jnp.sum(expon, axis=2)
        weight = expon.astype(jnp.bfloat16)
        numer = jnp.einsum("htk,kd->thd", weight.astype(jnp.float32), value_win)
        outcome = (numer / jnp.transpose(total)[:, :, None]).astype(jnp.bfloat16)
        return outcome.reshape(TOK_DEV, HEADS * HEAD_DIM), top + jnp.log(total)

    outcome, log_part = lax.map(one_device, jnp.arange(devices, dtype=jnp.int32))
    attended = outcome.reshape(SEQ, HEADS * HEAD_DIM)
    log_total = jnp.transpose(log_part, (1, 0, 2)).reshape(HEADS, SEQ)
    return attended, log_total
```

```python
import functools
import math

import jax
import jax.numpy as jnp
from jax import lax
from jax.experimental import pallas as pl
from jax.experimental.pallas import tpu as pltpu
from jax.sharding import PartitionSpec as P

AXES = ("outer", "inner")
LANES = 128
FAR = 2.0**15
NEG = -2.0**20
TILE = 128
HEADS_AT_ONCE = 2


def _inside(bounds, rows, offset, shape):
    at = lax.broadcasted_iota(jnp.int32, (rows, LANES), 0) + offset
    return (at >= bounds[0:1, :]) & (at < bounds[1:2, :])


def _dot_t(a, b):
    return lax.dot_general(a, b, (((1,), (1,)), ((), ())), preferred_element_type=jnp.float32)


def _stage(pieces, opens, closes, heads_here, scale, *refs):
    refs = list(refs)
    parity, bounds, q_ref = refs[:3]
    refs = refs[3:]
    rows = q_ref.shape[0]
    size = LANES
    n_blocks = len(pieces["steps"])
    kv = refs[:n_blocks]
    refs = refs[n_blocks:]
    if not opens:
        num_in, log_in = refs[:2]
        refs = refs[2:]
    num_out, log_out, key_s, val_s, doc_s = refs
    step = pl.program_id(0)

    @pl.when(step == 0)
    def _():
        b = bounds[...]
        mine = _inside(b, rows, 0, None)
        doc_s[...] = jnp.where(mine, -FAR, 0.0).astype(jnp.bfloat16)
        even = parity[0] == 0
        for n, back in enumerate(pieces["steps"]):
            here = pl.ds(n * rows, rows)
            if n_blocks == 2:
                one, two = kv[n], kv[1 - n]
                block = jnp.where(even, one[...], two[...])
            else:
                block = kv[n][...]
            key_s[here, 0:size] = block[0:rows]
            val_s[here, :] = block[rows : 2 * rows]
            theirs = _inside(b, rows, -back * rows, None)
            key_s[here, size : 2 * size] = jnp.where(theirs, 0.0, 1.0).astype(jnp.bfloat16)
        log_out[...] = jnp.zeros_like(log_out)

    tri = lax.broadcasted_iota(jnp.int32, (TILE, TILE), 0) - lax.broadcasted_iota(jnp.int32, (TILE, TILE), 1)
    lane = lax.broadcasted_iota(jnp.int32, (TILE, LANES), 1)

    def scores(i):
        rs = slice(i * TILE, (i + 1) * TILE)
        docs = doc_s[rs, :]
        left = jnp.concatenate(
            [
                jnp.concatenate([q_ref[rs, h * size : (h + 1) * size], docs], axis=1)
                for h in range(heads_here)
            ],
            axis=0,
        )
        start, count, _ = pieces["tiles"][i]
        return _dot_t(left, key_s[start : start + count, :])

    def finish(i, score):
        rs = slice(i * TILE, (i + 1) * TILE)
        start, count, edge = pieces["tiles"][i]
        out = []
        score = score.reshape(heads_here, TILE, count)
        if edge is not None:
            at, upper = edge
            keep = tri < 0 if upper else tri >= 0
            part = jnp.where(keep[None], score[:, :, at : at + TILE], NEG)
            parts = []
            if at:
                parts.append(score[:, :, :at])
            parts.append(part)
            if at + TILE < count:
                parts.append(score[:, :, at + TILE :])
            score = jnp.concatenate(parts, axis=2) if len(parts) > 1 else part
        top = jnp.max(score, axis=2, keepdims=True) * scale
        if not opens:
            logs = log_in[rs, :]
            before = jnp.stack(
                [
                    jnp.sum(jnp.where(lane == step * heads_here + h, logs, 0.0), axis=1, keepdims=True)
                    for h in range(heads_here)
                ]
            )
            top = jnp.maximum(top, before)
        expon = jnp.exp2(score * scale - top)
        total = jnp.sum(expon, axis=2, keepdims=True)
        weight = expon.astype(jnp.bfloat16).reshape(heads_here * TILE, count)
        num = jnp.dot(weight, val_s[start : start + count, :], preferred_element_type=jnp.float32)
        num = num.reshape(heads_here, TILE, size)
        if not opens:
            share = jnp.exp2(before - top)
            total = total + share
            for h in range(heads_here):
                out.append(num[h] + share[h] * num_in[rs, h * size : (h + 1) * size])
        else:
            out = [num[h] for h in range(heads_here)]
        inverse = 1.0 / total
        logs = top + jnp.log2(total)
        new = log_out[rs, :]
        for h in range(heads_here):
            num_out[rs, h * size : (h + 1) * size] = (out[h] * inverse[h]).astype(num_out.dtype)
            new = jnp.where(lane == step * heads_here + h, logs[h], new)
        log_out[rs, :] = new

    n = rows // TILE
    score = scores(0)
    for i in range(n):
        following = scores(i + 1) if i + 1 < n else None
        finish(i, score)
        score = following


def _call(name, pieces, parity, bounds, queries, kv, state, out_type):
    rows, width = queries.shape
    heads = width // LANES
    here = min(HEADS_AT_ONCE, heads)
    opens, closes = state is None, out_type == jnp.bfloat16
    scale = LANES**-0.5 * math.log2(math.e)
    whole = lambda x: pl.BlockSpec(x.shape, lambda s: (0, 0))
    wide = pl.BlockSpec((rows, here * LANES), lambda s: (0, s))
    logs = pl.BlockSpec((rows, LANES), lambda s: (0, 0))
    n = len(kv)
    count = sum(t[1] for t in pieces["tiles"]) * TILE * heads
    return pl.pallas_call(
        functools.partial(_stage, pieces, opens, closes, here, scale),
        grid=(heads // here,),
        in_specs=[pl.BlockSpec(memory_space=pltpu.SMEM), whole(bounds), wide]
        + [whole(x) for x in kv]
        + ([] if opens else [wide, logs]),
        out_specs=[wide, logs],
        out_shape=[
            jax.ShapeDtypeStruct((rows, width), out_type),
            jax.ShapeDtypeStruct((rows, LANES), jnp.float32),
        ],
        scratch_shapes=[
            pltpu.VMEM((n * rows, 2 * LANES), jnp.bfloat16),
            pltpu.VMEM((n * rows, LANES), jnp.bfloat16),
            pltpu.VMEM((rows, LANES), jnp.bfloat16),
        ],
        compiler_params=pltpu.CompilerParams(
            dimension_semantics=("arbitrary",), vmem_limit_bytes=48 * 1024 * 1024
        ),
        cost_estimate=pl.CostEstimate(
            flops=4 * count * LANES, bytes_accessed=6 * rows * width, transcendentals=count
        ),
        name=name,
    )(parity, bounds, queries, *kv, *(state or ()))


def shards(queries, keys, values, doc_lengths):
    rows = keys.shape[0]
    count = lax.axis_size("outer") * lax.axis_size("inner")
    me = lax.axis_index("outer") * lax.axis_size("inner") + lax.axis_index("inner")
    parity = (me % 2).astype(jnp.int32).reshape(1)
    n_docs = doc_lengths.shape[0]
    order = jnp.arange(n_docs)
    before = jnp.where(order[:, None] < jnp.arange(LANES)[None, :], doc_lengths[:, None], 0)
    starts = jnp.sum(before, axis=0)
    upto = jnp.where(order[:, None] <= jnp.arange(LANES)[None, :], doc_lengths[:, None], 0)
    ends = jnp.sum(upto, axis=0)
    bounds = jnp.concatenate([starts[None], ends[None]]).astype(jnp.int32) - me * rows

    def send(block, step_of):
        return lax.ppermute(
            block, AXES, [(i, i + step_of(i)) for i in range(count) if i + step_of(i) < count]
        )

    kv = jnp.concatenate([keys, values], axis=0)
    first = send(kv, lambda i: 1 if i % 2 else 3)
    second = send(kv, lambda i: 3 if i % 2 else 1)
    middle = send(first, lambda i: -1 if i % 2 else 1)

    n = rows // TILE
    own = {"steps": (0,), "tiles": [(0, (i + 1) * TILE, (i * TILE, False)) for i in range(n)]}
    sides = {"steps": (1, 3), "tiles": [(0, 0, None)] * n}
    sides = {
        "steps": (3, 1),
        "tiles": [(i * TILE, 2 * rows - i * TILE, (0, True)) for i in range(n)],
    }
    mid = {"steps": (2,), "tiles": [(0, rows, None)] * n}
    state = _call("own", own, parity, bounds, queries, [kv], None, jnp.float32)
    state = _call("sides", sides, parity, bounds, queries, [second, first], state, jnp.float32)
    attended, logs = _call("middle", mid, parity, bounds, queries, [middle], state, jnp.bfloat16)
    log_total = jnp.transpose(logs[:, : queries.shape[1] // LANES]) * math.log(2.0)
    return attended, log_total


def solution(mesh):
    placed = (P(AXES, None), P(AXES, None), P(AXES, None), P())
    return jax.shard_map(
        shards,
        mesh=mesh,
        in_specs=placed,
        out_specs=(P(AXES, None), P(None, AXES)),
        check_vma=False,
    )
```

```python
import functools
import math

import jax
import jax.numpy as jnp
from jax import lax
from jax.experimental import pallas as pl
from jax.experimental.pallas import tpu as pltpu
from jax.sharding import PartitionSpec as P

AXES = ("outer", "inner")
LANES = 128
SIZE = 128
FAR = 2.0**15
LEAST, MOST = 2.0**-60, 2.0**100
TILE = 128
SCALE = SIZE**-0.5 * math.log2(math.e)
VMEM_BYTES = 32 * 1024 * 1024


def _dot_t(a, b):
    return lax.dot_general(a, b, (((1,), (1,)), ((), ())), preferred_element_type=jnp.float32)


def _document_ends(me, lengths, rows):
    lane = lax.broadcasted_iota(jnp.int32, (1, LANES), 1)
    at = -me[0] * rows
    first = jnp.full((1, LANES), 0, jnp.int32)
    last = first
    for d in range(lengths.shape[0]):
        first = jnp.where(lane == d, at, first)
        at = at + lengths[d]
        last = jnp.where(lane == d, at, last)
    return first, last


def _inside(ends, rows, offset):
    at = lax.broadcasted_iota(jnp.int32, (rows, LANES), 0) + offset
    return (at >= ends[0]) & (at < ends[1])


def _scores(q_ref, doc_s, key_s, i, tile, here):
    rs = slice(i * TILE, (i + 1) * TILE)
    start, count, _ = tile
    docs = doc_s[rs, :]
    left = [jnp.concatenate([q_ref[rs, h * SIZE : (h + 1) * SIZE], docs], axis=1) for h in range(here)]
    return _dot_t(jnp.concatenate(left, axis=0), key_s[start : start + count, :])


def _weigh(score, val_s, tile, here):
    start, count, (at, upper) = tile
    expon = jnp.exp2(score * SCALE).reshape(here, TILE, count)
    tri = lax.broadcasted_iota(jnp.int32, (1, TILE, TILE), 1) - lax.broadcasted_iota(jnp.int32, (1, TILE, TILE), 2)
    parts = [expon[:, :, :at]] if at else []
    parts.append(jnp.where(tri < 0 if upper else tri >= 0, expon[:, :, at : at + TILE], 0.0))
    if at + TILE < count:
        parts.append(expon[:, :, at + TILE :])
    expon = jnp.concatenate(parts, axis=2).reshape(here * TILE, count)
    total = jnp.sum(expon, axis=1, keepdims=True)
    num = jnp.dot(expon.astype(jnp.bfloat16), val_s[start : start + count, :], preferred_element_type=jnp.float32)
    return num, total


def _wide(x, g, width):
    return x.at[:, pl.ds(pl.multiple_of(g * width, width), width)]


def _own(me, lengths, q, k, v, num, sum_out, doc_out, q_s, num_s, key_s, val_s, doc_s, sums, sem_q, sem_n, sem):
    groups, rows, width = q_s.shape
    here = width // SIZE

    def copy_q(g):
        return pltpu.make_async_copy(_wide(q, g, width), q_s.at[g], sem_q.at[g])

    def copy_n(g):
        return pltpu.make_async_copy(num_s.at[g], _wide(num, g, width), sem_n.at[g])

    copy_k = pltpu.make_async_copy(k, key_s.at[:, 0:SIZE], sem.at[0])
    copy_v = pltpu.make_async_copy(v, val_s, sem.at[1])
    copy_d = pltpu.make_async_copy(doc_s, doc_out, sem.at[2])
    copy_s = pltpu.make_async_copy(sums, sum_out, sem.at[3])
    for copy in [copy_k, copy_v] + [copy_q(g) for g in range(groups)]:
        copy.start()
    ends = _document_ends(me, lengths, rows)
    for n in range(3):
        theirs = _inside(ends, rows, (n - 3) * rows)
        doc_s[n * rows : (n + 1) * rows, :] = jnp.where(theirs, 0.0, 1.0).astype(jnp.bfloat16)
    mine = _inside(ends, rows, 0)
    doc_s[3 * rows :, :] = jnp.where(mine, -FAR, 0.0).astype(jnp.bfloat16)
    copy_d.start()
    key_s[:, SIZE:] = jnp.where(mine, 0.0, 1.0).astype(jnp.bfloat16)
    sums[...] = jnp.zeros_like(sums)
    copy_k.wait()
    copy_v.wait()

    lane = lax.broadcasted_iota(jnp.int32, (TILE, LANES), 1)
    n = rows // TILE
    tiles = [(0, (i + 1) * TILE, (i * TILE, False)) for i in range(n)]
    docs = doc_s.at[3 * rows :]

    def group(g, carry):
        copy_q(g).wait()
        score = _scores(q_s.at[g], docs, key_s, 0, tiles[0], here)
        for i in range(n):
            following = _scores(q_s.at[g], docs, key_s, i + 1, tiles[i + 1], here) if i + 1 < n else None
            part, total = _weigh(score, val_s, tiles[i], here)
            rs = slice(i * TILE, (i + 1) * TILE)
            new = sums[rs, :]
            for h in range(here):
                hs = slice(h * TILE, (h + 1) * TILE)
                num_s[g, rs, h * SIZE : (h + 1) * SIZE] = part[hs]
                new = jnp.where(lane == g * here + h, total[hs], new)
            sums[rs, :] = new
            score = following
        copy_n(g).start()
        return carry

    lax.fori_loop(0, groups, group, 0)
    copy_s.start()
    for g in range(groups):
        copy_n(g).wait()
    copy_d.wait()
    copy_s.wait()


def _again(me, lengths, q_s, key_s, val_s, out_s, logs):
    groups, rows, width = q_s.shape
    ends = _document_ends(me, lengths, rows)
    depth, reach = 4 * rows, 3 * rows
    lane = lax.broadcasted_iota(jnp.int32, (TILE, LANES), 1)

    def tile(i, carry):
        rs = pl.ds(pl.multiple_of(i * TILE, TILE), TILE)
        begin = jnp.sum(jnp.where(_inside(ends, TILE, i * TILE), ends[0], 0), axis=1, keepdims=True)
        row = lax.broadcasted_iota(jnp.int32, (TILE, depth), 0) + i * TILE
        key = lax.broadcasted_iota(jnp.int32, (TILE, depth), 1) - reach
        allowed = (key <= row) & (row - key < reach) & (key >= begin)

        def group(g, carry):
            for h in range(width // SIZE):
                cols = slice(h * SIZE, (h + 1) * SIZE)
                score = _dot_t(q_s[g, rs, cols], key_s[...]) * SCALE
                score = jnp.where(allowed, score, -jnp.inf)
                top = jnp.max(score, axis=1, keepdims=True)
                expon = jnp.exp2(score - top)
                total = jnp.sum(expon, axis=1, keepdims=True)
                num = jnp.dot(expon.astype(jnp.bfloat16), val_s[...], preferred_element_type=jnp.float32)
                out_s[g, rs, cols] = (num / total).astype(out_s.dtype)
                mine = lane == g * (width // SIZE) + h
                logs[rs, :] = jnp.where(mine, top + jnp.log2(total), logs[rs, :])
            return carry

        return lax.fori_loop(0, groups, group, carry)

    lax.fori_loop(0, rows // TILE, tile, 0)


def _rest(me, lengths, q, chip, second, num, sum_in, docs, own_k, own_v, out, last,
          q_s, num_s, out_s, last_s, key_s, val_s, doc_s, sums, logs, sem_q, sem_n, sem_o, sem_k, sem_v, sem_d):
    groups, rows, width = q_s.shape
    here = width // SIZE
    even = lax.rem(me[0], 2) == 0
    places = [jnp.where(even, 2, 1), jnp.where(even, 1, 0), jnp.where(even, 0, 2)]
    at = [pl.ds(pl.multiple_of(place * rows, rows), rows) for place in places]
    blocks = (chip.at[0], chip.at[1], second)
    copy_k = [pltpu.make_async_copy(x.at[:, 0:SIZE], key_s.at[w], sem_k.at[n]) for n, (x, w) in enumerate(zip(blocks, at))]
    copy_v = [pltpu.make_async_copy(x.at[:, SIZE:], val_s.at[w], sem_v.at[n]) for n, (x, w) in enumerate(zip(blocks, at))]
    copy_d = [pltpu.make_async_copy(docs, doc_s, sem_d.at[0]), pltpu.make_async_copy(sum_in, sums, sem_d.at[1])]

    def copy_q(g):
        return pltpu.make_async_copy(_wide(q, g, width), q_s.at[g], sem_q.at[g])

    def copy_n(g):
        return pltpu.make_async_copy(_wide(num, g, width), num_s.at[g], sem_n.at[g])

    def copy_o(g):
        return pltpu.make_async_copy(out_s.at[g], _wide(out, g, width), sem_o.at[g])

    for copy in copy_k + copy_d[:1] + [copy_q(0)] + copy_v + copy_d[1:] + [copy_n(0)]:
        copy.start()
    for g in range(1, groups):
        copy_q(g).start()
        copy_n(g).start()
    for copy in copy_k + copy_d + copy_v:
        copy.wait()

    lane = lax.broadcasted_iota(jnp.int32, (TILE, LANES), 1)
    n = rows // TILE
    tiles = [(i * TILE, 3 * rows - i * TILE, (0, True)) for i in range(n)]

    def scores(g, i):
        start, count, _ = tiles[i]
        rs, keys = slice(i * TILE, (i + 1) * TILE), slice(start, start + count)
        mine = doc_s[3 * rows + i * TILE : 3 * rows + (i + 1) * TILE, :]
        left = [jnp.concatenate([q_s[g, rs, h * SIZE : (h + 1) * SIZE], mine], axis=1) for h in range(here)]
        right = jnp.concatenate([key_s[keys, :], doc_s[keys, :]], axis=1)
        return _dot_t(jnp.concatenate(left, axis=0), right)

    def group(g, carry):
        copy_q(g).wait()
        score = scores(g, 0)
        copy_n(g).wait()
        for i in range(n):
            following = scores(g, i + 1) if i + 1 < n else None
            part, total = _weigh(score, val_s, tiles[i], here)
            rs = slice(i * TILE, (i + 1) * TILE)
            new = sums[rs, :]
            for h in range(here):
                hs, cols = slice(h * TILE, (h + 1) * TILE), slice(h * SIZE, (h + 1) * SIZE)
                mine = lane == g * here + h
                whole = total[hs] + jnp.sum(jnp.where(mine, new, 0.0), axis=1, keepdims=True)
                out_s[g, rs, cols] = ((part[hs] + num_s[g, rs, cols]) * (1.0 / whole)).astype(out_s.dtype)
                new = jnp.where(mine, whole, new)
            sums[rs, :] = new
            score = following
        copy_o(g).start()
        return carry

    lax.fori_loop(0, groups, group, 0)

    heads = last.shape[0]
    copy_l = pltpu.make_async_copy(last_s, last, sem_d.at[0])
    total = sums[...]
    last_s[...] = jnp.transpose(jnp.log(total))[0:heads, :]
    copy_l.start()
    fine = (total >= LEAST) & (total <= MOST)
    used = lax.broadcasted_iota(jnp.int32, total.shape, 1) < heads
    wrong = jnp.max(jnp.where(used & jnp.logical_not(fine), 1.0, 0.0))
    for g in range(groups):
        copy_o(g).wait()
    copy_l.wait()

    @pl.when(wrong > 0.0)
    def _():
        own = pl.ds(3 * rows, rows)
        copies = [
            pltpu.make_async_copy(own_k, key_s.at[own], sem_k.at[0]),
            pltpu.make_async_copy(own_v, val_s.at[own], sem_v.at[0]),
        ]
        for copy in copies:
            copy.start()
        for copy in copies:
            copy.wait()
        _again(me, lengths, q_s, key_s, val_s, out_s, logs)
        last_s[...] = jnp.transpose(logs[...])[0:heads, :] * math.log(2.0)
        copy_l.start()
        for g in range(groups):
            copy_o(g).start()
        for g in range(groups):
            copy_o(g).wait()
        copy_l.wait()


SCALARS = pl.BlockSpec(memory_space=pltpu.SMEM)
ANYWHERE = pl.BlockSpec(memory_space=pl.ANY)
HBM = pl.BlockSpec(memory_space=pltpu.HBM)


def _join(k, v, both, sem):
    copies = [pltpu.make_async_copy(x, both.at[:, n * SIZE : (n + 1) * SIZE], sem.at[n]) for n, x in enumerate((k, v))]
    for copy in copies:
        copy.start()
    for copy in copies:
        copy.wait()


def _join_call(keys, values):
    rows, size = keys.shape
    return pl.pallas_call(
        _join,
        in_specs=[HBM, HBM],
        out_specs=ANYWHERE,
        out_shape=jax.ShapeDtypeStruct((rows, 2 * size), keys.dtype),
        scratch_shapes=[pltpu.SemaphoreType.DMA((2,))],
        compiler_params=pltpu.CompilerParams(vmem_limit_bytes=1024 * 1024),
        cost_estimate=pl.CostEstimate(flops=0, bytes_accessed=8 * rows * size, transcendentals=0),
        name="join",
    )(keys, values)


def _own_call(me, lengths, queries, keys, values, here):
    rows, width = queries.shape
    heads = width // SIZE
    groups = heads // here
    pairs = heads * rows * (rows + TILE) // 2
    return pl.pallas_call(
        _own,
        in_specs=[SCALARS, SCALARS, HBM, HBM, HBM],
        out_specs=[ANYWHERE] * 3,
        out_shape=[
            jax.ShapeDtypeStruct((rows, width), jnp.float32),
            jax.ShapeDtypeStruct((rows, LANES), jnp.float32),
            jax.ShapeDtypeStruct((4 * rows, LANES), jnp.bfloat16),
        ],
        scratch_shapes=[
            pltpu.VMEM((groups, rows, here * SIZE), jnp.bfloat16),
            pltpu.VMEM((groups, rows, here * SIZE), jnp.float32),
            pltpu.VMEM((rows, SIZE + LANES), jnp.bfloat16),
            pltpu.VMEM((rows, SIZE), jnp.bfloat16),
            pltpu.VMEM((4 * rows, LANES), jnp.bfloat16),
            pltpu.VMEM((rows, LANES), jnp.float32),
            pltpu.SemaphoreType.DMA((groups,)),
            pltpu.SemaphoreType.DMA((groups,)),
            pltpu.SemaphoreType.DMA((4,)),
        ],
        compiler_params=pltpu.CompilerParams(vmem_limit_bytes=VMEM_BYTES),
        cost_estimate=pl.CostEstimate(flops=4 * pairs * SIZE, bytes_accessed=6 * rows * width, transcendentals=pairs),
        name="own",
    )(me, lengths, queries, keys, values)


def _rest_call(me, lengths, queries, blocks, state, keys, values, here):
    rows, width = queries.shape
    heads = width // SIZE
    groups = heads // here
    pairs = heads * rows * (5 * rows + TILE) // 2
    return pl.pallas_call(
        _rest,
        in_specs=[SCALARS, SCALARS, HBM] + [ANYWHERE] * 5 + [HBM] * 2,
        out_specs=[HBM, HBM],
        out_shape=[
            jax.ShapeDtypeStruct((rows, width), queries.dtype),
            jax.ShapeDtypeStruct((heads, rows), jnp.float32),
        ],
        scratch_shapes=[
            pltpu.VMEM((groups, rows, here * SIZE), jnp.bfloat16),
            pltpu.VMEM((groups, rows, here * SIZE), jnp.float32),
            pltpu.VMEM((groups, rows, here * SIZE), jnp.bfloat16),
            pltpu.VMEM((heads, rows), jnp.float32),
            pltpu.VMEM((4 * rows, SIZE), jnp.bfloat16),
            pltpu.VMEM((4 * rows, SIZE), jnp.bfloat16),
            pltpu.VMEM((4 * rows, LANES), jnp.bfloat16),
            pltpu.VMEM((rows, LANES), jnp.float32),
            pltpu.VMEM((rows, LANES), jnp.float32),
            pltpu.SemaphoreType.DMA((groups,)),
            pltpu.SemaphoreType.DMA((groups,)),
            pltpu.SemaphoreType.DMA((groups,)),
            pltpu.SemaphoreType.DMA((3,)),
            pltpu.SemaphoreType.DMA((3,)),
            pltpu.SemaphoreType.DMA((2,)),
        ],
        compiler_params=pltpu.CompilerParams(vmem_limit_bytes=VMEM_BYTES),
        cost_estimate=pl.CostEstimate(flops=4 * pairs * SIZE, bytes_accessed=8 * rows * width, transcendentals=pairs),
        name="rest",
    )(me, lengths, queries, *blocks, *state, keys, values)


def shards(queries, keys, values, doc_lengths):
    count = lax.axis_size("outer") * lax.axis_size("inner")
    me = (lax.axis_index("outer") * lax.axis_size("inner") + lax.axis_index("inner")).astype(jnp.int32).reshape(1)

    def send(block, step_of):
        return lax.ppermute(
            block, AXES, [(i, i + step_of(i)) for i in range(count) if i + step_of(i) < count]
        )

    both = _join_call(keys, values)
    first = send(both, lambda i: 1 if i % 2 else 3)
    second = send(both, lambda i: 3 if i % 2 else 1)
    state = _own_call(me, doc_lengths, queries, keys, values, 2)
    first, state = lax.optimization_barrier((first, state))
    chip = lax.all_gather(first, AXES, axis_index_groups=[[i, i + 1] for i in range(0, count, 2)])
    blocks = (chip, second)
    return tuple(_rest_call(me, doc_lengths, queries, blocks, state, keys, values, 2))


def solution(mesh):
    placed = (P(AXES, None), P(AXES, None), P(AXES, None), P())
    return jax.shard_map(
        shards,
        mesh=mesh,
        in_specs=placed,
        out_specs=(P(AXES, None), P(None, AXES)),
        check_vma=False,
    )
```

```python
import functools
import math

import jax
import jax.numpy as jnp
from jax import lax
from jax.experimental import pallas as pl
from jax.experimental.pallas import tpu as pltpu
from jax.sharding import PartitionSpec as P

AXES = ("outer", "inner")
LANES = 128
SIZE = 128
FAR = 2.0**15
LEAST, MOST = 2.0**-60, 2.0**100
TILE = 128
SCALE = SIZE**-0.5 * math.log2(math.e)
VMEM_BYTES = 32 * 1024 * 1024


def _dot_t(a, b):
    return lax.dot_general(a, b, (((1,), (1,)), ((), ())), preferred_element_type=jnp.float32)


def _document_ends(me, lengths, rows):
    lane = lax.broadcasted_iota(jnp.int32, (1, LANES), 1)
    at = -me[0] * rows
    first = jnp.full((1, LANES), 0, jnp.int32)
    last = first
    for d in range(lengths.shape[0]):
        first = jnp.where(lane == d, at, first)
        at = at + lengths[d]
        last = jnp.where(lane == d, at, last)
    return first, last


def _inside(ends, rows, offset):
    at = lax.broadcasted_iota(jnp.int32, (rows, LANES), 0) + offset
    return (at >= ends[0]) & (at < ends[1])


def _scores(q_ref, doc_s, key_s, i, tile, here):
    rs = slice(i * TILE, (i + 1) * TILE)
    start, count, _ = tile
    docs = doc_s[rs, :]
    left = [jnp.concatenate([q_ref[rs, h * SIZE : (h + 1) * SIZE], docs], axis=1) for h in range(here)]
    return _dot_t(jnp.concatenate(left, axis=0), key_s[start : start + count, :])


def _weigh(score, val_s, tile, here):
    start, count, (at, upper) = tile
    expon = jnp.exp2(score * SCALE).reshape(here, TILE, count)
    tri = lax.broadcasted_iota(jnp.int32, (1, TILE, TILE), 1) - lax.broadcasted_iota(jnp.int32, (1, TILE, TILE), 2)
    parts = [expon[:, :, :at]] if at else []
    parts.append(jnp.where(tri < 0 if upper else tri >= 0, expon[:, :, at : at + TILE], 0.0))
    if at + TILE < count:
        parts.append(expon[:, :, at + TILE :])
    expon = jnp.concatenate(parts, axis=2).reshape(here * TILE, count)
    num = jnp.dot(expon.astype(jnp.bfloat16), val_s[start : start + count, :], preferred_element_type=jnp.float32)
    return num[:, 0:SIZE], num[:, SIZE:]


def _own(me, lengths, q, both, num, sums, docs, key_s, val_s):
    rows, width = q.shape
    here = width // SIZE
    n = rows // TILE
    ends = _document_ends(me, lengths, rows)
    for back in range(3):
        theirs = _inside(ends, rows, (back - 3) * rows)
        docs[back * rows : (back + 1) * rows, :] = jnp.where(theirs, 0.0, 1.0).astype(jnp.bfloat16)
    mine = _inside(ends, rows, 0)
    docs[3 * rows :, :] = jnp.where(mine, -FAR, 0.0).astype(jnp.bfloat16)
    key_s[:, 0:SIZE] = both[:, 0:SIZE]
    key_s[:, SIZE:] = jnp.where(mine, 0.0, 1.0).astype(jnp.bfloat16)
    val_s[:, 0:SIZE] = both[:, SIZE:]
    val_s[:, SIZE:] = jnp.ones((rows, LANES), jnp.bfloat16)

    lane = lax.broadcasted_iota(jnp.int32, (TILE, LANES), 1)
    tiles = [(0, (i + 1) * TILE, (i * TILE, False)) for i in range(n)]
    my_docs = docs.at[3 * rows :]
    score = _scores(q, my_docs, key_s, 0, tiles[0], here)
    for i in range(n):
        rs = slice(i * TILE, (i + 1) * TILE)
        following = _scores(q, my_docs, key_s, i + 1, tiles[i + 1], here) if i + 1 < n else None
        part, total = _weigh(score, val_s, tiles[i], here)
        new = jnp.zeros((TILE, LANES), jnp.float32)
        for h in range(here):
            hs = slice(h * TILE, (h + 1) * TILE)
            num[rs, h * SIZE : (h + 1) * SIZE] = part[hs]
            new = jnp.where(lane == h, total[hs], new)
        sums[rs, :] = new
        score = following


def _again(me, lengths, q, key_s, val_s, out_s, logs):
    rows, width = q.shape
    ends = _document_ends(me, lengths, rows)
    depth, reach = 4 * rows, 3 * rows
    lane = lax.broadcasted_iota(jnp.int32, (TILE, LANES), 1)

    def tile(i, carry):
        rs = pl.ds(pl.multiple_of(i * TILE, TILE), TILE)
        begin = jnp.sum(jnp.where(_inside(ends, TILE, i * TILE), ends[0], 0), axis=1, keepdims=True)
        row = lax.broadcasted_iota(jnp.int32, (TILE, depth), 0) + i * TILE
        key = lax.broadcasted_iota(jnp.int32, (TILE, depth), 1) - reach
        allowed = (key <= row) & (row - key < reach) & (key >= begin)

        def head(h, carry):
            cols = pl.ds(pl.multiple_of(h * SIZE, SIZE), SIZE)
            score = _dot_t(q[rs, cols], key_s[...]) * SCALE
            score = jnp.where(allowed, score, -jnp.inf)
            top = jnp.max(score, axis=1, keepdims=True)
            expon = jnp.exp2(score - top)
            total = jnp.sum(expon, axis=1, keepdims=True)
            num = jnp.dot(expon.astype(jnp.bfloat16), val_s[:, 0:SIZE], preferred_element_type=jnp.float32)
            out_s[rs, cols] = (num / total).astype(out_s.dtype)
            logs[rs, :] = jnp.where(lane == h, top + jnp.log2(total), logs[rs, :])
            return carry

        return lax.fori_loop(0, width // SIZE, head, carry)

    lax.fori_loop(0, rows // TILE, tile, 0)


def _rest(me, lengths, q, chip, second, num, sums, docs, both, out, last,
          out_s, last_s, key_s, val_s, logs, sem_o, sem_k, sem_v, sem_l):
    rows, width = q.shape
    here = width // SIZE
    n = rows // TILE
    even = lax.rem(me[0], 2) == 0
    places = [jnp.where(even, 2, 1), jnp.where(even, 1, 0), jnp.where(even, 0, 2)]
    at = [pl.ds(pl.multiple_of(place * rows, rows), rows) for place in places]
    blocks = (chip.at[0], chip.at[1], second)
    copy_k = [pltpu.make_async_copy(x.at[:, 0:SIZE], key_s.at[w], sem_k.at[j]) for j, (x, w) in enumerate(zip(blocks, at))]
    copy_v = [
        pltpu.make_async_copy(x.at[:, SIZE:], val_s.at[w, 0:SIZE], sem_v.at[j]) for j, (x, w) in enumerate(zip(blocks, at))
    ]
    spans = [slice(i * TILE, (i + 1) * TILE) for i in range(n)]
    copy_o = [pltpu.make_async_copy(out_s.at[rs], out.at[rs], sem_o.at[i]) for i, rs in enumerate(spans)]
    copy_l = pltpu.make_async_copy(last_s, last, sem_l)
    for copy in copy_k + copy_v:
        copy.start()
    val_s[0 : 3 * rows, SIZE:] = jnp.ones((3 * rows, LANES), jnp.bfloat16)
    for copy in copy_k + copy_v:
        copy.wait()

    lane = lax.broadcasted_iota(jnp.int32, (TILE, LANES), 1)
    tiles = [(i * TILE, 3 * rows - i * TILE, (0, True)) for i in range(n)]

    def scores(i):
        start, count, _ = tiles[i]
        rs, keys = spans[i], slice(start, start + count)
        mine = docs[3 * rows + i * TILE : 3 * rows + (i + 1) * TILE, :]
        left = [jnp.concatenate([q[rs, h * SIZE : (h + 1) * SIZE], mine], axis=1) for h in range(here)]
        right = jnp.concatenate([key_s[keys, :], docs[keys, :]], axis=1)
        return _dot_t(jnp.concatenate(left, axis=0), right)

    score = scores(0)
    for i, rs in enumerate(spans):
        following = scores(i + 1) if i + 1 < n else None
        part, total = _weigh(score, val_s, tiles[i], here)
        before = sums[rs, :]
        log = jnp.zeros((TILE, LANES), jnp.float32)
        for h in range(here):
            hs, cols = slice(h * TILE, (h + 1) * TILE), slice(h * SIZE, (h + 1) * SIZE)
            whole = total[hs] + jnp.broadcast_to(before[:, h : h + 1], (TILE, LANES))
            out_s[rs, cols] = ((part[hs] + num[rs, cols]) * (1.0 / whole)).astype(out_s.dtype)
            log = jnp.where(lane == h, whole, log)
        logs[rs, :] = log
        copy_o[i].start()
        score = following

    heads = last.shape[0]
    total = logs[...]
    last_s[...] = jnp.transpose(jnp.log(total))[0:heads, :]
    copy_l.start()
    fine = (total >= LEAST) & (total <= MOST)
    used = lax.broadcasted_iota(jnp.int32, total.shape, 1) < heads
    wrong = jnp.max(jnp.where(used & jnp.logical_not(fine), 1.0, 0.0))
    for copy in copy_o + [copy_l]:
        copy.wait()

    @pl.when(wrong > 0.0)
    def _():
        own = pl.ds(3 * rows, rows)
        copies = [
            pltpu.make_async_copy(both.at[:, 0:SIZE], key_s.at[own], sem_k.at[0]),
            pltpu.make_async_copy(both.at[:, SIZE:], val_s.at[own, 0:SIZE], sem_v.at[0]),
        ]
        for copy in copies:
            copy.start()
        for copy in copies:
            copy.wait()
        _again(me, lengths, q, key_s, val_s, out_s, logs)
        last_s[...] = jnp.transpose(logs[...])[0:heads, :] * math.log(2.0)
        for copy in copy_o + [copy_l]:
            copy.start()
        for copy in copy_o + [copy_l]:
            copy.wait()


SCALARS = pl.BlockSpec(memory_space=pltpu.SMEM)
ANYWHERE = pl.BlockSpec(memory_space=pl.ANY)
HBM = pl.BlockSpec(memory_space=pltpu.HBM)
VMEM = pl.BlockSpec(memory_space=pltpu.VMEM)


def _join(k, v, both, sem):
    copies = [pltpu.make_async_copy(x, both.at[:, n * SIZE : (n + 1) * SIZE], sem.at[n]) for n, x in enumerate((k, v))]
    for copy in copies:
        copy.start()
    for copy in copies:
        copy.wait()


def _join_call(keys, values):
    rows, size = keys.shape
    return pl.pallas_call(
        _join,
        in_specs=[HBM, HBM],
        out_specs=ANYWHERE,
        out_shape=jax.ShapeDtypeStruct((rows, 2 * size), keys.dtype),
        scratch_shapes=[pltpu.SemaphoreType.DMA((2,))],
        compiler_params=pltpu.CompilerParams(vmem_limit_bytes=1024 * 1024),
        cost_estimate=pl.CostEstimate(flops=0, bytes_accessed=8 * rows * size, transcendentals=0),
        name="join",
    )(keys, values)


def _own_call(me, lengths, queries, both):
    rows, width = queries.shape
    pairs = width // SIZE * rows * (rows + TILE) // 2
    return pl.pallas_call(
        _own,
        in_specs=[SCALARS, SCALARS, VMEM, VMEM],
        out_specs=[VMEM] * 3,
        out_shape=[
            jax.ShapeDtypeStruct((rows, width), jnp.float32),
            jax.ShapeDtypeStruct((rows, LANES), jnp.float32),
            jax.ShapeDtypeStruct((4 * rows, LANES), jnp.bfloat16),
        ],
        scratch_shapes=[
            pltpu.VMEM((rows, SIZE + LANES), jnp.bfloat16),
            pltpu.VMEM((rows, SIZE + LANES), jnp.bfloat16),
        ],
        compiler_params=pltpu.CompilerParams(vmem_limit_bytes=VMEM_BYTES),
        cost_estimate=pl.CostEstimate(flops=4 * pairs * SIZE, bytes_accessed=6 * rows * width, transcendentals=pairs),
        name="own",
    )(me, lengths, queries, both)


def _rest_call(me, lengths, queries, blocks, state, both):
    rows, width = queries.shape
    heads = width // SIZE
    pairs = heads * rows * (5 * rows + TILE) // 2
    return pl.pallas_call(
        _rest,
        in_specs=[SCALARS, SCALARS, VMEM, ANYWHERE, ANYWHERE, VMEM, VMEM, VMEM, ANYWHERE],
        out_specs=[HBM, HBM],
        out_shape=[
            jax.ShapeDtypeStruct((rows, width), queries.dtype),
            jax.ShapeDtypeStruct((heads, rows), jnp.float32),
        ],
        scratch_shapes=[
            pltpu.VMEM((rows, width), jnp.bfloat16),
            pltpu.VMEM((heads, rows), jnp.float32),
            pltpu.VMEM((4 * rows, SIZE), jnp.bfloat16),
            pltpu.VMEM((4 * rows, SIZE + LANES), jnp.bfloat16),
            pltpu.VMEM((rows, LANES), jnp.float32),
            pltpu.SemaphoreType.DMA((rows // TILE,)),
            pltpu.SemaphoreType.DMA((3,)),
            pltpu.SemaphoreType.DMA((3,)),
            pltpu.SemaphoreType.DMA,
        ],
        compiler_params=pltpu.CompilerParams(vmem_limit_bytes=VMEM_BYTES),
        cost_estimate=pl.CostEstimate(flops=4 * pairs * SIZE, bytes_accessed=8 * rows * width, transcendentals=pairs),
        name="rest",
    )(me, lengths, queries, *blocks, *state, both)


def shards(queries, keys, values, doc_lengths):
    count = lax.axis_size("outer") * lax.axis_size("inner")
    me = (lax.axis_index("outer") * lax.axis_size("inner") + lax.axis_index("inner")).astype(jnp.int32).reshape(1)

    def send(block, step_of):
        return lax.ppermute(
            block, AXES, [(i, i + step_of(i)) for i in range(count) if i + step_of(i) < count]
        )

    both = _join_call(*(pltpu.with_memory_space_constraint(x, pltpu.HBM) for x in (keys, values)))
    first = send(both, lambda i: 1 if i % 2 else 3)
    second = send(both, lambda i: 3 if i % 2 else 1)
    state = _own_call(me, doc_lengths, queries, both)
    first, state = lax.optimization_barrier((first, state))
    chip = lax.all_gather(first, AXES, axis_index_groups=[[i, i + 1] for i in range(0, count, 2)])
    blocks = (chip, second)
    return tuple(_rest_call(me, doc_lengths, queries, blocks, state, both))


def solution(mesh):
    placed = (P(AXES, None), P(AXES, None), P(AXES, None), P())
    return jax.shard_map(
        shards,
        mesh=mesh,
        in_specs=placed,
        out_specs=(P(AXES, None), P(None, AXES)),
        check_vma=False,
    )
```

```python
import functools
import math

import jax
import jax.numpy as jnp
from jax import lax
from jax.experimental import pallas as pl
from jax.experimental.pallas import tpu as pltpu
from jax.sharding import PartitionSpec as P

AXES = ("outer", "inner")
LANES = 128
SIZE = 128
FAR = 2.0**15
LEAST, MOST = 2.0**-60, 2.0**100
TILE = 128
SCALE = SIZE**-0.5 * math.log2(math.e)
VMEM_BYTES = 32 * 1024 * 1024


def _dot_t(a, b):
    return lax.dot_general(a, b, (((1,), (1,)), ((), ())), preferred_element_type=jnp.float32)


def _document_ends(me, lengths, rows):
    lane = lax.broadcasted_iota(jnp.int32, (1, LANES), 1)
    at = -me[0] * rows
    first = jnp.full((1, LANES), 0, jnp.int32)
    last = first
    for d in range(lengths.shape[0]):
        first = jnp.where(lane == d, at, first)
        at = at + lengths[d]
        last = jnp.where(lane == d, at, last)
    return first, last


def _inside(ends, rows, offset):
    at = lax.broadcasted_iota(jnp.int32, (rows, LANES), 0) + offset
    return (at >= ends[0]) & (at < ends[1])


def _scores(q_ref, doc_s, key_s, i, tile, here):
    rs = slice(i * TILE, (i + 1) * TILE)
    start, count, _ = tile
    docs = doc_s[rs, :]
    left = [jnp.concatenate([q_ref[rs, h * SIZE : (h + 1) * SIZE], docs], axis=1) for h in range(here)]
    return _dot_t(jnp.concatenate(left, axis=0), key_s[start : start + count, :])


def _weigh(score, val_s, tile, here):
    start, count, (at, upper) = tile
    expon = jnp.exp2(score * SCALE).reshape(here, TILE, count)
    tri = lax.broadcasted_iota(jnp.int32, (1, TILE, TILE), 1) - lax.broadcasted_iota(jnp.int32, (1, TILE, TILE), 2)
    parts = [expon[:, :, :at]] if at else []
    parts.append(jnp.where(tri < 0 if upper else tri >= 0, expon[:, :, at : at + TILE], 0.0))
    if at + TILE < count:
        parts.append(expon[:, :, at + TILE :])
    expon = jnp.concatenate(parts, axis=2).reshape(here * TILE, count)
    num = jnp.dot(expon.astype(jnp.bfloat16), val_s[start : start + count, :], preferred_element_type=jnp.float32)
    return num[:, 0:SIZE], num[:, SIZE:]


def _own(me, lengths, q, both, num, sums, docs, key_s, val_s):
    rows, width = q.shape
    here = width // SIZE
    n = rows // TILE
    ends = _document_ends(me, lengths, rows)
    for back in range(3):
        theirs = _inside(ends, rows, (back - 3) * rows)
        docs[back * rows : (back + 1) * rows, :] = jnp.where(theirs, 0.0, 1.0).astype(jnp.bfloat16)
    mine = _inside(ends, rows, 0)
    docs[3 * rows :, :] = jnp.where(mine, -FAR, 0.0).astype(jnp.bfloat16)
    key_s[:, 0:SIZE] = both[:, 0:SIZE]
    key_s[:, SIZE:] = jnp.where(mine, 0.0, 1.0).astype(jnp.bfloat16)
    val_s[:, 0:SIZE] = both[:, SIZE:]
    val_s[:, SIZE:] = jnp.ones((rows, LANES), jnp.bfloat16)

    lane = lax.broadcasted_iota(jnp.int32, (TILE, LANES), 1)
    tiles = [(0, (i + 1) * TILE, (i * TILE, False)) for i in range(n)]
    my_docs = docs.at[3 * rows :]
    score = _scores(q, my_docs, key_s, 0, tiles[0], here)
    for i in range(n):
        rs = slice(i * TILE, (i + 1) * TILE)
        following = _scores(q, my_docs, key_s, i + 1, tiles[i + 1], here) if i + 1 < n else None
        part, total = _weigh(score, val_s, tiles[i], here)
        new = jnp.zeros((TILE, LANES), jnp.float32)
        for h in range(here):
            hs = slice(h * TILE, (h + 1) * TILE)
            num[rs, h * SIZE : (h + 1) * SIZE] = part[hs]
            new = jnp.where(lane == h, total[hs], new)
        sums[rs, :] = new
        score = following


def _again(me, lengths, q, key_s, val_s, out_s, logs):
    rows, width = q.shape
    ends = _document_ends(me, lengths, rows)
    depth, reach = 4 * rows, 3 * rows
    lane = lax.broadcasted_iota(jnp.int32, (TILE, LANES), 1)

    def tile(i, carry):
        rs = pl.ds(pl.multiple_of(i * TILE, TILE), TILE)
        begin = jnp.sum(jnp.where(_inside(ends, TILE, i * TILE), ends[0], 0), axis=1, keepdims=True)
        row = lax.broadcasted_iota(jnp.int32, (TILE, depth), 0) + i * TILE
        key = lax.broadcasted_iota(jnp.int32, (TILE, depth), 1) - reach
        allowed = (key <= row) & (row - key < reach) & (key >= begin)

        def head(h, carry):
            cols = pl.ds(pl.multiple_of(h * SIZE, SIZE), SIZE)
            score = _dot_t(q[rs, cols], key_s[...]) * SCALE
            score = jnp.where(allowed, score, -jnp.inf)
            top = jnp.max(score, axis=1, keepdims=True)
            expon = jnp.exp2(score - top)
            total = jnp.sum(expon, axis=1, keepdims=True)
            num = jnp.dot(expon.astype(jnp.bfloat16), val_s[:, 0:SIZE], preferred_element_type=jnp.float32)
            out_s[rs, cols] = (num / total).astype(out_s.dtype)
            logs[rs, :] = jnp.where(lane == h, top + jnp.log2(total), logs[rs, :])
            return carry

        return lax.fori_loop(0, width // SIZE, head, carry)

    lax.fori_loop(0, rows // TILE, tile, 0)


def _rest(me, lengths, q, chip, second, late, num, sums, docs, both, out, last,
          out_s, last_s, key_s, val_s, logs, sem_o, sem_k, sem_v, sem_l):
    rows, width = q.shape
    here = width // SIZE
    n = rows // TILE
    even = lax.rem(me[0], 2) == 0
    places = [jnp.where(even, 2, 1), jnp.where(even, 1, 0), jnp.where(even, 0, 2)]
    at = [pl.ds(pl.multiple_of(place * rows, rows), rows) for place in places]
    blocks = (chip.at[0], chip.at[1], second)
    copy_k = [pltpu.make_async_copy(x.at[:, 0:SIZE], key_s.at[w], sem_k.at[j]) for j, (x, w) in enumerate(zip(blocks, at))]
    copy_v = [
        pltpu.make_async_copy(x.at[:, SIZE:], val_s.at[w, 0:SIZE], sem_v.at[j]) for j, (x, w) in enumerate(zip(blocks, at))
    ]
    spans = [slice(i * TILE, (i + 1) * TILE) for i in range(n)]
    copy_o = [pltpu.make_async_copy(out_s.at[rs], out.at[rs], sem_o.at[i]) for i, rs in enumerate(spans)]
    copy_l = pltpu.make_async_copy(last_s, last, sem_l)
    is_late = me[0] == me[1]

    @pl.when(is_late)
    def _():
        pltpu.make_async_copy(late.at[:, 0:SIZE], key_s.at[at[2]], sem_k.at[2]).start()
        pltpu.make_async_copy(late.at[:, SIZE:], val_s.at[at[2], 0:SIZE], sem_v.at[2]).start()

    @pl.when(jnp.logical_not(is_late))
    def _():
        copy_k[2].start()
        copy_v[2].start()

    for copy in copy_k[:2] + copy_v[:2]:
        copy.start()
    val_s[0 : 3 * rows, SIZE:] = jnp.ones((3 * rows, LANES), jnp.bfloat16)
    for copy in copy_k + copy_v:
        copy.wait()

    lane = lax.broadcasted_iota(jnp.int32, (TILE, LANES), 1)
    tiles = [(i * TILE, 3 * rows - i * TILE, (0, True)) for i in range(n)]

    def scores(i):
        start, count, _ = tiles[i]
        rs, keys = spans[i], slice(start, start + count)
        mine = docs[3 * rows + i * TILE : 3 * rows + (i + 1) * TILE, :]
        left = [jnp.concatenate([q[rs, h * SIZE : (h + 1) * SIZE], mine], axis=1) for h in range(here)]
        right = jnp.concatenate([key_s[keys, :], docs[keys, :]], axis=1)
        return _dot_t(jnp.concatenate(left, axis=0), right)

    score = scores(0)
    for i, rs in enumerate(spans):
        following = scores(i + 1) if i + 1 < n else None
        part, total = _weigh(score, val_s, tiles[i], here)
        before = sums[rs, :]
        log = jnp.zeros((TILE, LANES), jnp.float32)
        for h in range(here):
            hs, cols = slice(h * TILE, (h + 1) * TILE), slice(h * SIZE, (h + 1) * SIZE)
            whole = total[hs] + jnp.broadcast_to(before[:, h : h + 1], (TILE, LANES))
            out_s[rs, cols] = ((part[hs] + num[rs, cols]) * (1.0 / whole)).astype(out_s.dtype)
            log = jnp.where(lane == h, whole, log)
        logs[rs, :] = log
        copy_o[i].start()
        score = following

    heads = last.shape[0]
    total = logs[...]
    last_s[...] = jnp.transpose(jnp.log(total))[0:heads, :]
    copy_l.start()
    fine = (total >= LEAST) & (total <= MOST)
    used = lax.broadcasted_iota(jnp.int32, total.shape, 1) < heads
    wrong = jnp.max(jnp.where(used & jnp.logical_not(fine), 1.0, 0.0))
    for copy in copy_o + [copy_l]:
        copy.wait()

    @pl.when(wrong > 0.0)
    def _():
        own = pl.ds(3 * rows, rows)
        copies = [
            pltpu.make_async_copy(both.at[:, 0:SIZE], key_s.at[own], sem_k.at[0]),
            pltpu.make_async_copy(both.at[:, SIZE:], val_s.at[own, 0:SIZE], sem_v.at[0]),
        ]
        for copy in copies:
            copy.start()
        for copy in copies:
            copy.wait()
        _again(me, lengths, q, key_s, val_s, out_s, logs)
        last_s[...] = jnp.transpose(logs[...])[0:heads, :] * math.log(2.0)
        for copy in copy_o + [copy_l]:
            copy.start()
        for copy in copy_o + [copy_l]:
            copy.wait()


SCALARS = pl.BlockSpec(memory_space=pltpu.SMEM)
ANYWHERE = pl.BlockSpec(memory_space=pl.ANY)
HBM = pl.BlockSpec(memory_space=pltpu.HBM)
VMEM = pl.BlockSpec(memory_space=pltpu.VMEM)


def _join(k, v, both, sem):
    copies = [pltpu.make_async_copy(x, both.at[:, n * SIZE : (n + 1) * SIZE], sem.at[n]) for n, x in enumerate((k, v))]
    for copy in copies:
        copy.start()
    for copy in copies:
        copy.wait()


def _join_call(keys, values):
    rows, size = keys.shape
    return pl.pallas_call(
        _join,
        in_specs=[HBM, HBM],
        out_specs=ANYWHERE,
        out_shape=jax.ShapeDtypeStruct((rows, 2 * size), keys.dtype),
        scratch_shapes=[pltpu.SemaphoreType.DMA((2,))],
        compiler_params=pltpu.CompilerParams(vmem_limit_bytes=1024 * 1024),
        cost_estimate=pl.CostEstimate(flops=0, bytes_accessed=8 * rows * size, transcendentals=0),
        name="join",
    )(keys, values)


def _own_call(me, lengths, queries, both):
    rows, width = queries.shape
    pairs = width // SIZE * rows * (rows + TILE) // 2
    return pl.pallas_call(
        _own,
        in_specs=[SCALARS, SCALARS, VMEM, VMEM],
        out_specs=[VMEM] * 3,
        out_shape=[
            jax.ShapeDtypeStruct((rows, width), jnp.float32),
            jax.ShapeDtypeStruct((rows, LANES), jnp.float32),
            jax.ShapeDtypeStruct((4 * rows, LANES), jnp.bfloat16),
        ],
        scratch_shapes=[
            pltpu.VMEM((rows, SIZE + LANES), jnp.bfloat16),
            pltpu.VMEM((rows, SIZE + LANES), jnp.bfloat16),
        ],
        compiler_params=pltpu.CompilerParams(vmem_limit_bytes=VMEM_BYTES),
        cost_estimate=pl.CostEstimate(flops=4 * pairs * SIZE, bytes_accessed=6 * rows * width, transcendentals=pairs),
        name="own",
    )(me, lengths, queries, both)


def _rest_call(me, lengths, queries, blocks, state, both):
    rows, width = queries.shape
    heads = width // SIZE
    pairs = heads * rows * (5 * rows + TILE) // 2
    return pl.pallas_call(
        _rest,
        in_specs=[SCALARS, SCALARS, VMEM, ANYWHERE, ANYWHERE, ANYWHERE, VMEM, VMEM, VMEM, ANYWHERE],
        out_specs=[HBM, HBM],
        out_shape=[
            jax.ShapeDtypeStruct((rows, width), queries.dtype),
            jax.ShapeDtypeStruct((heads, rows), jnp.float32),
        ],
        scratch_shapes=[
            pltpu.VMEM((rows, width), jnp.bfloat16),
            pltpu.VMEM((heads, rows), jnp.float32),
            pltpu.VMEM((4 * rows, SIZE), jnp.bfloat16),
            pltpu.VMEM((4 * rows, SIZE + LANES), jnp.bfloat16),
            pltpu.VMEM((rows, LANES), jnp.float32),
            pltpu.SemaphoreType.DMA((rows // TILE,)),
            pltpu.SemaphoreType.DMA((3,)),
            pltpu.SemaphoreType.DMA((3,)),
            pltpu.SemaphoreType.DMA,
        ],
        compiler_params=pltpu.CompilerParams(vmem_limit_bytes=VMEM_BYTES),
        cost_estimate=pl.CostEstimate(flops=4 * pairs * SIZE, bytes_accessed=8 * rows * width, transcendentals=pairs),
        name="rest",
    )(me, lengths, queries, *blocks, *state, both)


def shards(queries, keys, values, doc_lengths):
    count = lax.axis_size("outer") * lax.axis_size("inner")
    me = (lax.axis_index("outer") * lax.axis_size("inner") + lax.axis_index("inner")).astype(jnp.int32)
    me = jnp.stack([me, jnp.int32(count // 2)])

    def send(block, step_of, chosen=lambda i: True):
        pairs = [(i, i + step_of(i)) for i in range(count) if i + step_of(i) < count and chosen(i)]
        return lax.ppermute(block, AXES, pairs)

    first = [send(x, lambda i: 1 if i % 2 else 3) for x in (keys, values)]
    both = _join_call(*(pltpu.with_memory_space_constraint(x, pltpu.HBM) for x in (keys, values)))
    late = send(both, lambda i: 3 if i % 2 else 1, lambda i: i == count // 2 - 3)
    second = send(both, lambda i: 3 if i % 2 else 1, lambda i: i != count // 2 - 3)
    state = _own_call(me, doc_lengths, queries, both)
    first, state = lax.optimization_barrier((first, state))
    first = jnp.concatenate(first, axis=1)
    chip = lax.all_gather(first, AXES, axis_index_groups=[[i, i + 1] for i in range(0, count, 2)])
    blocks = (chip, second, late)
    return tuple(_rest_call(me, doc_lengths, queries, blocks, state, both))


def solution(mesh):
    placed = (P(AXES, None), P(AXES, None), P(AXES, None), P())
    return jax.shard_map(
        shards,
        mesh=mesh,
        in_specs=placed,
        out_specs=(P(AXES, None), P(None, AXES)),
        check_vma=False,
    )
```
